128 devices in a mesh: fr: 8 (over x, core), fc: 8 (over z_lo, y), cam: 2 (over z_hi).
Axes of the slice: x: 4, y: 4, z: 4 (z_hi: 2, z_lo: 2; z = z_hi * 2 + z_lo), core: 2. Of those that a mesh axis runs over, the one named last changes fastest.
Arguments:
- view_a: bfloat16 [4096, 8192], P(('fc', 'cam'), 'fr'), may hold values from -64 to 64
- view_b: bfloat16 [4096, 8192], P(('fr', 'cam'), 'fc'), may hold values from -64 to 64
Outputs:
- grad_a: bfloat16 [4096, 8192], P(('fc', 'cam'), 'fr')
- grad_b: bfloat16 [4096, 8192], P(('fr', 'cam'), 'fc')
- loss: float32 [], replicated
The draws below stay inside these ranges and needn't reach their ends.
All inputs are finite; a program needn't handle non-finite values.
Results may differ from the reference program's by a relative error of at most 0.011.
Values may be sent and summed in bfloat16 or wider, within the bound.
No kernel may reach another device: no remote copies, remote signals or barrier semaphores. Data moves between devices by JAX's collectives and lax.ppermute only.
A program may use at most 128 MiB of HBM per device.

```python
import math
import jax
import jax.numpy as jnp
from jax import lax

FEAT = 8192
CLIPS = 4096


def shared_parts(key, ceiling):
    keys = jax.random.split(key, 3)
    latent = jnp.clip(jax.random.normal(keys[0], (CLIPS, FEAT), jnp.float32), -4.0, 4.0)
    feature_pos = lax.broadcasted_iota(jnp.float32, (1, FEAT), 1) / max(FEAT - 1, 1)
    gap = (0.03 + 0.12 * feature_pos) * jax.random.uniform(keys[1], (1, FEAT), jnp.float32, 0.5, 1.0)
    spread = jnp.sqrt(gap / (1.0 - gap))
    power = 1.0 + 0.4 * feature_pos
    position = lax.broadcasted_iota(jnp.float32, (CLIPS, 1), 0) / max(CLIPS - 1, 1)
    level = 0.5 * position + 0.5 * jax.random.uniform(keys[2], (CLIPS, 1), jnp.float32)
    row_scale = jnp.exp(level * math.log(ceiling) * power)
    return (latent, spread, row_scale)


def build_view(key, parts, jitter, offset_range):
    latent, spread, row_scale = parts
    keys = jax.random.split(key, 2)
    col_scale = jnp.exp(jax.random.uniform(keys[0], (1, FEAT), jnp.float32, math.log(0.02), math.log(0.2)))
    offset = jax.random.uniform(keys[1], (1, FEAT), jnp.float32, -offset_range, offset_range)
    values = col_scale * row_scale * (latent + spread * jitter) + offset
    return jnp.clip(values, -64.0, 64.0)


def draw_view_a(key, part):
    parts = shared_parts(key, 10.0)
    key = jax.random.fold_in(key, 11)
    jitter_key = jax.random.fold_in(key, 5)
    jitter = jnp.clip(jax.random.normal(jitter_key, (CLIPS, FEAT), jnp.float32), -5.0, 5.0)
    offset_range = 0.5
    return build_view(key, parts, jitter, offset_range).astype(jnp.bfloat16)


def draw_view_b(key, part):
    parts = shared_parts(key, 10.0)
    key = jax.random.fold_in(key, 23)
    jitter_key = jax.random.fold_in(key, 7)
    jitter = jnp.clip(jax.random.normal(jitter_key, (CLIPS, FEAT), jnp.float32), -5.0, 5.0)
    offset_range = 0.5
    return build_view(key, parts, jitter, offset_range).astype(jnp.bfloat16)


def setup_inputs(seed: int = 0) -> dict:
    key_of = jax.random.split(jax.random.key(seed), 3)
    return {
        "view_a": draw_view_a(jax.random.fold_in(key_of[2], 71), 0),
        "view_b": draw_view_b(jax.random.fold_in(key_of[2], 71), 0),
    }


EPSILON = 1e-05
WEIGHT_SCALE = 42.0

def normalize(view):
    values = view.astype(jnp.float32)
    column_mean = lax.optimization_barrier(jnp.mean(values, axis=0))
    column_msq = lax.optimization_barrier(jnp.mean(values * values, axis=0))
    scale = lax.rsqrt(column_msq - column_mean * column_mean + EPSILON)
    return (((values - column_mean) * scale).astype(jnp.bfloat16), scale)

def backward(back, normed, scale):
    normal_f = normed.astype(jnp.float32)
    first = lax.optimization_barrier(jnp.mean(back, axis=0))
    second = lax.optimization_barrier(jnp.mean(back * normal_f, axis=0))
    return (scale * (back - first - normal_f * second)).astype(jnp.bfloat16)

def reference(view_a, view_b):
    norm_a, scale_a = normalize(view_a)
    norm_b, scale_b = normalize(view_b)
    correlation = lax.dot_general(norm_a, norm_b, (((0,), (0,)), ((), ())), preferred_element_type=jnp.float32) / CLIPS
    identity_mask = jnp.eye(FEAT, dtype=bool)
    weight = WEIGHT_SCALE / FEAT
    diagonal = jnp.diagonal(correlation)
    off_terms = jnp.sum(jnp.where(identity_mask, jnp.float32(0.0), correlation * correlation))
    loss = (jnp.sum((1.0 - diagonal) * (1.0 - diagonal)) + weight * off_terms) / FEAT
    grad_corr = jnp.where(identity_mask, -2.0 * (1.0 - correlation), 2.0 * weight * correlation).astype(jnp.bfloat16)
    back_a = lax.dot_general(norm_b, grad_corr, (((1,), (1,)), ((), ())), preferred_element_type=jnp.float32)
    back_b = jnp.dot(norm_a, grad_corr, preferred_element_type=jnp.float32)
    return (backward(back_a, norm_a, scale_a), backward(back_b, norm_b, scale_b), loss)
```

```python
import functools

import jax
import jax.numpy as jnp
from jax import lax
from jax.experimental import pallas as pl
from jax.experimental.pallas import tpu as pltpu
from jax.sharding import PartitionSpec as P

FEAT = 8192
CLIPS = 4096
EPSILON = 1e-05
WEIGHT = 42.0 / FEAT

AXES = ("fr", "fc", "cam")
BLOCK = 256
HALF_A = 512
WIDE_B = 1024
STEPS = 4
VMEM_LIMIT = 56 * 1024 * 1024


def send(value, move):
    pairs = []
    for device in range(128):
        fr, fc, hi = device // 16, device // 2 % 8, device % 2
        x, core, y, lo, hi = move(fr // 2, fr % 2, fc % 4, fc // 4, hi)
        pairs.append((device, ((x % 4) * 2 + core) * 16 + (lo * 4 + y % 4) * 2 + hi))
    return lax.ppermute(value, AXES, pairs)


def ring_x(value):
    return send(value, lambda x, c, y, lo, hi: (x + 1 - 2 * c, c, y, lo, hi))


def ring_y(value):
    return send(value, lambda x, c, y, lo, hi: (x, c, y + 1 - 2 * c, lo, hi))


def swap_core(value):
    return send(value, lambda x, c, y, lo, hi: (x, 1 - c, y, lo, hi))


def swap_lo(value):
    return send(value, lambda x, c, y, lo, hi: (x, c, y, 1 - lo, hi))


def swap_near(value):
    return send(value, lambda x, c, y, lo, hi: (x, c, y, 1 - lo, 1 - hi))


def half_cam(value, first):
    return send(value, lambda x, c, y, lo, hi: (x, c, y, 1 - lo, hi if c != first else 1 - hi))


def tie(*values):
    return lax.optimization_barrier(values)


class Order:
    def __init__(self, value=None):
        self.last = value

    def __call__(self, value):
        if self.last is not None:
            value, _ = tie(value, self.last)
        self.last = value
        return value


def sublanes(values):
    rows, width = values.shape
    return jnp.sum(values.reshape(rows // 8, 8, width), axis=0)


def lane_groups(values):
    total = values[:, :128]
    for n in range(1, values.shape[1] // 128):
        total = total + values[:, n * 128 : (n + 1) * 128]
    return total


def split_rows(row):
    high = row.astype(jnp.bfloat16).astype(jnp.float32)
    mid = (row - high).astype(jnp.bfloat16).astype(jnp.float32)
    low = row - high - mid
    ids = lax.broadcasted_iota(jnp.int32, (16, row.shape[1]), 0)
    picked = jnp.where(ids == 0, high, jnp.where(ids == 1, mid, jnp.where(ids == 2, low, 0.0)))
    return picked.astype(jnp.bfloat16)


def statistics(ref, width):
    step = 256
    zero = jnp.zeros((8, width), jnp.float32)

    def add(k, carry):
        total, squares = carry
        values = ref[pl.ds(pl.multiple_of(k * step, step), step), :].astype(jnp.float32)
        return total + sublanes(values), squares + sublanes(values * values)

    total, squares = lax.fori_loop(0, CLIPS // step, add, (zero, zero))
    mean = jnp.sum(total, axis=0, keepdims=True) / CLIPS
    msq = jnp.sum(squares, axis=0, keepdims=True) / CLIPS
    return mean, lax.rsqrt(msq - mean * mean + EPSILON)


def normalize_rows(ref, rows, mean, scale):
    normed = ((ref[rows, :].astype(jnp.float32) - mean) * scale).astype(jnp.bfloat16)
    ref[rows, :] = normed
    return sublanes(normed.astype(jnp.float32))


def finish(back, normed, vec):
    back = back - vec[1:2, :] - normed.astype(jnp.float32) * vec[2:3, :]
    return (back * vec[0:1, :]).astype(jnp.bfloat16)


def row_sets(place, bases, k):
    first_a, first_b = place[bases["rows_a"] + k], place[bases["rows_b"] + 2 * k]
    own_b = place[bases["rows_b"] + 2 * k + 1]
    return [pl.multiple_of(start, 512) for start in (first_b, own_b, first_a, first_a + 2048)]


def product(n, place, bases, a_rows, b_rows, grad_ref, vec_a, vec_b, part_a, part_b):
    if n < 2:
        back = jnp.dot(a_rows[...], grad_ref[...], preferred_element_type=jnp.float32)
        value = finish(back, b_rows[...], vec_b)
        part, spots = part_b.at[pl.ds(n * 512, 512)], 4
    else:
        back = lax.dot_general(
            b_rows[...], grad_ref[...], (((1,), (1,)), ((), ())), preferred_element_type=jnp.float32
        )
        value = finish(back, a_rows[...], vec_a)
        part, spots = part_a, 2 * (n - 2)
    for half in range(2):
        spot = pl.multiple_of(place[bases["spot"] + spots + half], BLOCK)
        part[pl.ds(spot, BLOCK), :] = value[half * BLOCK : (half + 1) * BLOCK]
    return part


def front_kernel(plan_a, plan_b, bases, *refs):
    place = refs[0]
    count_a = 1 + max(p for p, *_ in plan_a)
    count_b = 1 + max(p for p, *_ in plan_b)
    pieces_a, pieces_b = refs[1 : 1 + count_a], refs[1 + count_a : 1 + count_a + count_b]
    refs = refs[1 + count_a + count_b :]
    twin, twins = refs[0:2]
    own, leave, stay, owns, leaves, stays, loss_ref = refs[2:9]
    a_ref, b_ref, c_ref, grad_ref, vec_a, vec_b, parts_a, parts_b = refs[9:17]
    sems_a, sems_b, sems_out = refs[17:]

    def copies(plan, pieces, whole, sems, base):
        made = []
        for n, (piece, start, rows, _) in enumerate(plan):
            target = pl.multiple_of(place[base + n], BLOCK)
            made.append(
                pltpu.make_async_copy(
                    pieces[piece].at[pl.ds(start, rows)],
                    whole.at[pl.ds(target, rows)],
                    sems.at[n],
                )
            )
        return made

    moves_a = copies(plan_a, pieces_a, a_ref, sems_a, bases["a"])
    moves_b = copies(plan_b, pieces_b, b_ref, sems_b, bases["b"])
    for move in moves_a + moves_b:
        move.start()
    for move in moves_a:
        move.wait()
    mean_a, scale_a = statistics(a_ref, HALF_A)
    for move in moves_b:
        move.wait()
    mean_b, scale_b = statistics(b_ref, WIDE_B)

    step = 1024
    sums_a = jnp.zeros((8, HALF_A), jnp.float32)
    sums_b = jnp.zeros((8, WIDE_B), jnp.float32)
    for k in range(CLIPS // step):
        rows = pl.ds(k * step, step)
        sums_a += normalize_rows(a_ref, rows, mean_a, scale_a)
        sums_b += normalize_rows(b_ref, rows, mean_b, scale_b)
        part = lax.dot_general(
            a_ref[rows, :],
            b_ref[rows, :],
            (((0,), (0,)), ((), ())),
            preferred_element_type=jnp.float32,
        )
        if k == 0:
            c_ref[...] = part
        else:
            c_ref[...] += part
    mean_a = jnp.sum(sums_a, axis=0, keepdims=True) / CLIPS
    mean_b = jnp.sum(sums_b, axis=0, keepdims=True) / CLIPS

    first_id = place[bases["id"]]
    rows = 128
    zero = jnp.zeros((8, WIDE_B), jnp.float32)
    loss, second_b = zero, zero
    for k in range(HALF_A // rows):
        corr = c_ref[pl.ds(k * rows, rows), :] * (1.0 / CLIPS)
        ids = lax.broadcasted_iota(jnp.int32, (rows, WIDE_B), 0) + (first_id + k * rows)
        on_diag = ids == lax.broadcasted_iota(jnp.int32, (rows, WIDE_B), 1)
        missing = 1.0 - corr
        loss += sublanes(jnp.where(on_diag, missing * missing, WEIGHT * corr * corr))
        grad = jnp.where(on_diag, -2.0 * missing, 2.0 * WEIGHT * corr).astype(jnp.bfloat16)
        grad_ref[pl.ds(k * rows, rows), :] = grad
        second = grad.astype(jnp.float32) * corr
        second_b += sublanes(second)
        vec_a[2:3, pl.ds(k * rows, rows)] = jnp.sum(lane_groups(second).T, axis=0, keepdims=True)
    loss_ref[...] = lane_groups(loss)
    first_a = lax.dot_general(
        split_rows(mean_b),
        grad_ref[...],
        (((1,), (1,)), ((), ())),
        preferred_element_type=jnp.float32,
    )
    first_b = jnp.dot(split_rows(mean_a), grad_ref[...], preferred_element_type=jnp.float32)
    vec_a[0:1, :] = scale_a
    vec_a[1:2, :] = jnp.sum(first_a, axis=0, keepdims=True)
    vec_b[0:1, :] = scale_b
    vec_b[1:2, :] = jnp.sum(first_b, axis=0, keepdims=True)
    vec_b[2:3, :] = jnp.sum(second_b, axis=0, keepdims=True)

    def copies_out(k, targets):
        part_a, part_b = parts_a.at[k], parts_b.at[k]
        sources = [
            part_b.at[pl.ds(0, BLOCK)],
            part_b.at[pl.ds(BLOCK, BLOCK)],
            part_b.at[pl.ds(512, 512)],
            part_a.at[pl.ds(0, 512)],
            part_a.at[pl.ds(512, 512)],
        ]
        return [
            pltpu.make_async_copy(source, target, sems_out.at[5 * k + n])
            for n, (source, target) in enumerate(zip(sources, targets))
        ]

    def run_step(k, start_out):
        for n, start in enumerate(row_sets(place, bases, k)):
            rows = pl.ds(start, 512)
            product(
                n, place, bases, a_ref.at[rows], b_ref.at[rows], grad_ref, vec_a, vec_b,
                parts_a.at[k], parts_b.at[k],
            )
            start_out(n)

    def later_copies(k):
        rows = pl.ds((k - 1) * 512, 512)
        early = k == STEPS - 1
        second = jnp.where(early, 1024, (k - 1) * 512 + BLOCK)
        second = pl.ds(pl.multiple_of(second, BLOCK), BLOCK)
        first = pl.ds(pl.multiple_of(jnp.where(early, 0, (k - 1) * 512), BLOCK), BLOCK)
        targets = [twins.at[first], twins.at[second], owns.at[rows], leaves.at[rows], stays.at[rows]]
        made = copies_out(k, targets)
        return made, copies_out(k, [twin.at[pl.ds(512, BLOCK)]])[0]

    first_copies = copies_out(
        0, [twin.at[pl.ds(0, BLOCK)], twin.at[pl.ds(BLOCK, BLOCK)], own, leave, stay]
    )

    def start_first(n):
        for copy in ((0, 1), (2,), (), (3, 4))[n]:
            first_copies[copy].start()

    run_step(0, start_first)

    def later(k, carry):
        made, early = later_copies(k)

        def start_later(n):
            if n == 0:

                @pl.when(k == STEPS - 1)
                def _():
                    early.start()

                @pl.when(k < STEPS - 1)
                def _():
                    made[0].start()

            for copy in ((1,), (2,), (), (3, 4))[n]:
                made[copy].start()

        run_step(k, start_later)
        return carry

    lax.fori_loop(1, STEPS, later, 0)
    for copy in first_copies:
        copy.wait()
    for k in range(1, STEPS):
        for copy in later_copies(jnp.int32(k))[0]:
            copy.wait()


ANY = pl.BlockSpec(memory_space=pl.ANY)
IN_VMEM = pl.BlockSpec(memory_space=pltpu.VMEM)
NARROW = jax.ShapeDtypeStruct((512, HALF_A), jnp.bfloat16)
WIDE = jax.ShapeDtypeStruct((512, WIDE_B), jnp.bfloat16)


def run_front(place, bases, pieces_a, pieces_b, plan_a, plan_b):
    out = pl.pallas_call(
        functools.partial(front_kernel, plan_a, plan_b, bases),
        out_shape=tuple(
            jax.ShapeDtypeStruct(shape, jnp.bfloat16)
            for shape in (
                (768, WIDE_B),
                (1280, WIDE_B),
                (512, WIDE_B),
                (512, HALF_A),
                (512, HALF_A),
                (1536, WIDE_B),
                (1536, HALF_A),
                (1536, HALF_A),
            )
        )
        + (jax.ShapeDtypeStruct((8, 128), jnp.float32),),
        in_specs=[pl.BlockSpec(memory_space=pltpu.SMEM)]
        + [ANY] * (len(pieces_a) + len(pieces_b)),
        out_specs=(ANY,) * 8 + (IN_VMEM,),
        scratch_shapes=[
            pltpu.VMEM((CLIPS, HALF_A), jnp.bfloat16),
            pltpu.VMEM((CLIPS, WIDE_B), jnp.bfloat16),
            pltpu.VMEM((HALF_A, WIDE_B), jnp.float32),
            pltpu.VMEM((HALF_A, WIDE_B), jnp.bfloat16),
            pltpu.VMEM((8, HALF_A), jnp.float32),
            pltpu.VMEM((8, WIDE_B), jnp.float32),
            pltpu.VMEM((STEPS, 1024, HALF_A), jnp.bfloat16),
            pltpu.VMEM((STEPS, 1024, WIDE_B), jnp.bfloat16),
            pltpu.SemaphoreType.DMA((len(plan_a),)),
            pltpu.SemaphoreType.DMA((len(plan_b),)),
            pltpu.SemaphoreType.DMA((5 * STEPS,)),
        ],
        compiler_params=pltpu.CompilerParams(vmem_limit_bytes=VMEM_LIMIT),
        cost_estimate=pl.CostEstimate(
            flops=6 * CLIPS * HALF_A * WIDE_B, bytes_accessed=24 << 20, transcendentals=0
        ),
        name="front",
    )(place, *pieces_a, *pieces_b)
    parts = [out[2:5]]
    for k in range(STEPS - 1):
        parts.append(tuple(whole[k * 512 : (k + 1) * 512] for whole in out[5:8]))
    return out[0], out[1], parts, out[8]


def add(*parts, to=jnp.bfloat16):
    total = parts[0].astype(jnp.float32)
    for part in parts[1:]:
        total = total + part.astype(jnp.float32)
    return total.astype(to)


def on_device(view_a, view_b):
    fr, fc, hi = lax.axis_index("fr"), lax.axis_index("fc"), lax.axis_index("cam")
    x, core, lo, y = fr // 2, fr % 2, fc // 4, fc % 4
    way = 1 - 2 * core

    left, right = view_a[:, :HALF_A], view_a[:, HALF_A:]
    other = jnp.where(hi == 0, right, left)
    mine = jnp.where(hi == 0, left, right)
    plan_a, plan_b = [], []
    spots = [(lo, hi), (1 - lo, hi), (1 - lo, 1 - hi), (lo, 1 - hi)]
    for n in range(2 * STEPS):
        y_at = (y - n % 4 * way) % 4
        for half in range(2):
            lo_at, hi_at = spots[n // 4 * 2 + half]
            row = ((lo_at * 4 + y_at) * 2 + hi_at) * BLOCK
            plan_a.append((n, half * BLOCK, BLOCK, row))
    for n in range(4 * STEPS):
        group, k = n // 4, n % 4
        core_at = core if group < 2 else 1 - core
        hi_at = hi if group % 2 == 0 else 1 - hi
        x_at = (x - k * (1 - 2 * core_at)) % 4
        plan_b.append((n, 0, BLOCK, ((x_at * 2 + core_at) * 2 + hi_at) * BLOCK))
    order_a = []
    for lo_at in range(2):
        for hi_at in range(2):
            same_lo, same_hi = lo == lo_at, hi == hi_at
            stays = same_lo == same_hi
            order_a.append((stays * 2 + same_lo) * BLOCK)
    order_b = [(hi == 0) * BLOCK, (hi == 1) * BLOCK]
    rows_a, rows_b = [], []
    for k in range(1, STEPS + 1):
        rows_a.append(((y - k * way) % 4) * 512)
        rows_b.append((((x + k * way) % 4) * 2 + 1 - core) * 512)
        rows_b.append((((x - k * way) % 4) * 2 + core) * 512)
    tables = {
        "a": [row for *_, row in plan_a],
        "b": [row for *_, row in plan_b],
        "id": [fr * 1024 + hi * HALF_A - fc * WIDE_B],
        "spot": order_a + order_b,
        "rows_a": rows_a,
        "rows_b": rows_b,
    }
    bases, flat = {}, []
    for name, table in tables.items():
        bases[name] = len(flat)
        flat += [jnp.asarray(value, jnp.int32) for value in table]
    place = jnp.stack(flat)

    then = Order()
    partner = half_cam(view_b, True)
    b_1, twin_0 = ring_x(view_b), swap_core(view_b)
    from_near = swap_near(other)
    from_lo = swap_lo(mine)
    partner = then(partner)
    partner = half_cam(partner, False)
    from_near = then(from_near)
    from_far = swap_lo(from_near)
    from_lo = then(from_lo)
    a_0 = jnp.concatenate([mine, from_lo], axis=0)
    a_1 = ring_y(a_0)
    b_1 = then(b_1)
    b_2, twin_1 = ring_x(b_1), swap_core(b_1)
    twin_0 = then(twin_0)
    partner = then(partner)
    partner_1, twin_4 = ring_x(partner), swap_core(partner)
    from_far = then(from_far)
    others_0 = jnp.concatenate([from_near, from_far], axis=0)
    others_1 = ring_y(others_0)
    a_1 = then(a_1)
    a_2 = ring_y(a_1)
    b_2 = then(b_2)
    b_3, twin_2 = ring_x(b_2), swap_core(b_2)
    twin_1 = then(twin_1)
    partner_1 = then(partner_1)
    partner_2, twin_5 = ring_x(partner_1), swap_core(partner_1)
    others_1 = then(others_1)
    others_2 = ring_y(others_1)
    twin_4 = then(twin_4)
    a_2 = then(a_2)
    a_3 = ring_y(a_2)
    twin_2 = then(twin_2)
    place = then(place)
    b_3 = then(b_3)
    twin_3 = swap_core(b_3)
    partner_2 = then(partner_2)
    partner_3, twin_6 = ring_x(partner_2), swap_core(partner_2)
    others_2 = then(others_2)
    others_3 = ring_y(others_2)
    twin_5 = then(twin_5)
    a_3 = then(a_3)
    twin_3 = then(twin_3)
    twin_6 = then(twin_6)
    partner_3 = then(partner_3)
    twin_7 = swap_core(partner_3)
    others_3 = then(others_3)
    pieces_a = [a_0, a_1, a_2, a_3, others_0, others_1, others_2, others_3]
    pieces_b = [view_b, b_1, b_2, b_3, partner, partner_1, partner_2, partner_3]
    pieces_b += [twin_0, twin_1, twin_2, twin_3, twin_4, twin_5, twin_6, twin_7]

    twin, twins, parts, loss = run_front(place, bases, pieces_a, pieces_b, plan_a, plan_b)

    def total(value, hop):
        return value + hop(value)

    own, leave, stay = parts[0]
    twin = swap_core(twin)
    loss = total(loss, swap_lo)
    then = Order(loss)
    twin = then(twin)
    twins, _ = tie(twins, twin)
    twins = swap_core(twins)
    cross = add(own[:BLOCK], twin[:BLOCK])
    then.last = cross
    keep = add(own[BLOCK:], then(twin)[BLOCK:512])
    then.last = keep
    far = add(parts[STEPS - 1][0][:BLOCK], then(twin)[512:])
    then.last = far
    far = half_cam(far, True)
    last = parts[STEPS - 1]

    def chunk(k, rows):
        return parts[k][0][rows], then(twins)[(k - 1) * 512 : k * 512][rows]

    def hop(loss, move):
        loss, _ = tie(loss, then.last)
        loss = total(loss, move)
        then.last = loss
        return loss

    on, end = slice(BLOCK), slice(BLOCK, None)
    for k in (1, 2):
        cross, leave, keep, stay = ring_x(cross), ring_y(leave), ring_x(keep), ring_y(stay)
        if k == 1:
            loss = hop(loss, swap_core)
        cross = add(*chunk(k, on), then(cross))
        then.last = cross
        far = half_cam(then(far), False) if k == 1 else then(far)
        leave = add(parts[k][1], then(leave))
        then.last = leave
        if k == 1:
            keep = add(*chunk(k, end), then(keep))
            then.last = keep
            stay = add(parts[k][2], then(stay))
            then.last = stay
    cross = half_cam(cross, True)
    leave = ring_y(leave)
    keep = add(*chunk(2, end), then(keep), to=jnp.float32)
    then.last = keep
    stay = add(parts[2][2], then(stay))
    then.last = stay
    stay = ring_y(stay)
    loss = hop(loss, swap_near)
    cross = then(cross)
    cross = half_cam(cross, False)
    leave = then(leave)
    leave_on, leave_end = add(last[1][end], leave[end]), add(last[1][on], leave[on])
    arrived_on, arrived_end = swap_lo(leave_on), swap_lo(leave_end)
    then.last = leave_end
    loss = hop(loss, ring_x)
    stay = then(stay)
    loss = hop(loss, lambda value: send(value, lambda x, c, y, lo, hi: (x + 2, c, y, lo, hi)))
    near = add(last[2][on], stay[on], then(arrived_on))
    across = swap_near(near)
    then.last = near
    keep = add(keep, then(cross))
    then.last = keep
    keep = ring_x(keep)
    loss = hop(loss, ring_y)
    arrived_end = then(arrived_end)
    stays = add(last[2][end], stay[end], arrived_end)
    loss = hop(loss, lambda value: send(value, lambda x, c, y, lo, hi: (x, c, y + 2, lo, hi)))
    kept = add(last[0][end], then(twins)[1024:], far, to=jnp.float32)
    grad_a = jnp.where(
        hi == 0,
        jnp.concatenate([stays, across], axis=1),
        jnp.concatenate([across, stays], axis=1),
    )
    grad_b = add(kept, keep)
    return (grad_a, grad_b, jnp.sum(loss) / FEAT)


def solution(mesh):
    in_specs = (P(("fc", "cam"), "fr"), P(("fr", "cam"), "fc"))
    out_specs = (P(("fc", "cam"), "fr"), P(("fr", "cam"), "fc"), P())
    return jax.shard_map(
        on_device, mesh=mesh, in_specs=in_specs, out_specs=out_specs, check_vma=False
    )
```
